32 devices in a mesh: groups: 2 (over x), region: 16 (over z, y, core).
Axes of the slice: x: 2, y: 2, z: 4, core: 2. Of those that a mesh axis runs over, the one named last changes fastest.
Arguments:
- attributes: bfloat16 [16, 16384], P(None, 'region'), may hold values from -6 to 6
- w_in: bfloat16 [16, 512], replicated, may hold values from -1.5 to 1.5
- w_mid: bfloat16 [512, 512], replicated, may hold values from -0.25 to 0.25
- w_out: bfloat16 [2, 512], replicated, may hold values from -0.25 to 0.25
- b_hid: float32 [2, 512], replicated, may hold values from -3 to 3
- b_out: float32 [2], replicated, may hold values from -3 to 3
- downstream: int32 [16384], P('region'), may hold values from -1 to 16383, as said below
- lateral: float32 [4, 32768], P(None, ('groups', 'region')), parts along dimension 1, may hold values from 0.002 to 0.05
- flow_start: float32 [32768], P(('groups', 'region')), parts along dimension 0, may hold values from 0.1 to 2
- cotangent: float32 [4, 32768], P(None, ('groups', 'region')), parts along dimension 1, may hold values from -0.0625 to 0.0625
Outputs:
- flows: float32 [4, 32768], P(None, ('groups', 'region')), parts along dimension 1
- grad_in: float32 [32, 512], P('groups'), parts along dimension 0
- grad_mid: float32 [1024, 512], P('groups'), parts along dimension 0
- grad_out: float32 [4, 512], P('groups'), parts along dimension 0
- grad_bias: float32 [4, 512], P('groups'), parts along dimension 0
The draws below stay inside these ranges and needn't reach their ends.
There are 2 independent parts, one for each index of `groups`. The reference program is written for one: setup_inputs(seed, part) draws one part's arguments, and reference() takes and returns one part's arrays. A program takes and returns all parts, laid end to end along the dimension named above; an argument that names none is the same for every part. Nothing has to cross between parts.
Inputs may be any that keep to these rules, and one draw needn't show every extreme that they name: `downstream`: local reach k of each device (global index minus the device's first) lies in tier k // 64 of 16 tiers. A reach outside a device's last tier points to a reach of the same device 1 to 3 tiers later, or of the last tier; a reach of a device's last tier points to some reach of the next device, and on the last device it is an outlet, -1.
All inputs are finite; a program needn't handle non-finite values.
Results may differ from the reference program's by a relative error of at most 0.0056.
Values sent between devices are 32-bit elements; how exact they have to be, the bound alone decides.
A program may use at most 64 MiB of HBM per device.

```python
import math
import jax
import jax.numpy as jnp
from jax import lax

ATTR = 16
HID = 512
TIERS = 16
HOP = 3
STEPS = 4
R_DEV = 1024
REACHES = 16384


def draw_downstream(key, part):
    total = REACHES
    per_dev = R_DEV
    devices = total // per_dev
    exits = per_dev // TIERS
    index = jnp.arange(total, dtype=jnp.int32)
    device = index // per_dev
    local = index % per_dev
    tier = local // exits
    slot = local % exits
    key_jump = jax.random.fold_in(key, 11)
    key_slot = jax.random.fold_in(key, 23)
    key_entry = jax.random.fold_in(key, 37)
    jump = jax.random.randint(key_jump, (total,), 1, HOP + 1, dtype=jnp.int32)
    jump = jnp.where(slot == 0, 1, jnp.where(slot == 1, HOP, jump))
    to_tier = jnp.minimum(tier + jump, TIERS - 1)
    to_slot = jax.random.randint(key_slot, (total,), 0, exits, dtype=jnp.int32)
    to_slot = jnp.where(slot == 0, 0, to_slot)
    inner = device * per_dev + to_tier * exits + to_slot
    entry = jax.random.randint(key_entry, (total,), 0, per_dev, dtype=jnp.int32)
    entry = jnp.where(slot == 0, 0, jnp.where(slot == exits - 1, per_dev - 1, entry))
    onward = (device + 1) * per_dev + entry
    last_tier = tier == TIERS - 1
    result = jnp.where(last_tier, jnp.where(device == devices - 1, -1, onward), inner)
    return result.astype(jnp.int32)


def block_scale(rng, dims, cuts, smallest, top_value):
    def one(dim, parts):
        draws = jax.random.uniform(jax.random.fold_in(jax.random.fold_in(rng, 6), dim), (parts,), jnp.float32, smallest / len(cuts), top_value / len(cuts))
        return jnp.repeat(jnp.exp(draws), dims[dim] // parts).reshape((-1,) + (1,) * (len(dims) - dim - 1))

    gain = one(*cuts[0])
    for cut in cuts[1:]:
        gain = gain * one(*cut)
    return gain


def noise(rng, dims, spread, bound, split=(), kind=jnp.bfloat16):
    values = jax.random.normal(rng, dims, jnp.float32) * spread
    if len(split) > 0:
        values = block_scale(rng, dims, split, -0.22, 0.18) * values
    return jnp.clip(values, min=-bound, max=bound).astype(kind)


def setup_inputs(seed: int = 0, part: int = 0) -> dict:
    key_list = jax.random.split(jax.random.key(seed), 11)
    own_keys = jax.random.split(jax.random.fold_in(key_list[10], part), 11)
    attributes = noise(key_list[0], (ATTR, REACHES), 1.0, 6.0, ((1, 16),))
    w_in = noise(key_list[1], (ATTR, HID), ATTR ** -0.5, 1.5)
    w_mid = noise(key_list[2], (HID, HID), HID ** -0.5, 0.25)
    w_out = noise(key_list[3], (2, HID), HID ** -0.5, 0.25)
    b_hid = noise(key_list[4], (2, HID), 0.5, 3.0, (), jnp.float32)
    b_out = noise(key_list[5], (2,), 1.0, 3.0, (), jnp.float32)
    downstream = draw_downstream(jax.random.fold_in(key_list[10], 71), part)
    lateral = jnp.clip(jnp.exp(math.log(0.05) - 3.218876 * jax.random.uniform(own_keys[7], (STEPS, REACHES), jnp.float32) ** block_scale(own_keys[7], (STEPS, REACHES), ((1, 16),), -0.2, 0.2)), 0.002, 0.05)
    flow_start = jnp.clip(jnp.exp(math.log(2.0) - 2.9957323 * jax.random.uniform(own_keys[8], (REACHES,), jnp.float32) ** block_scale(own_keys[8], (REACHES,), ((0, 16),), -0.2, 0.2)), 0.1, 2.0)
    cotangent = noise(own_keys[9], (STEPS, REACHES), ((REACHES * STEPS) ** -0.5), 0.0625, ((1, 16),), jnp.float32)
    return {"attributes": attributes, "w_in": w_in, "w_mid": w_mid, "w_out": w_out, "b_hid": b_hid, "b_out": b_out, "downstream": downstream, "lateral": lateral, "flow_start": flow_start, "cotangent": cotangent}


RHO_LO = 16.0
RHO_HI = 16000.0

def coefficients(logits):
    rho = RHO_LO * jnp.exp(jnp.log(RHO_HI / RHO_LO) * jax.nn.sigmoid(logits[0]))
    weight = 0.45 * jax.nn.sigmoid(logits[1])
    denom = rho + 2.0 * (1.0 - weight)
    return ((rho - 2.0 * weight) / denom, (rho + 2.0 * weight) / denom, (2.0 * (1.0 - weight) - rho) / denom, 2.0 * rho / denom)

def silu_slope(pre):
    sig = jax.nn.sigmoid(pre)
    return sig * (1.0 + pre * (1.0 - sig))

def contract_last(left, right):
    return lax.dot_general(left, right, (((1,), (1,)), ((), ())), preferred_element_type=jnp.float32)

def layer_forward(block, w_in, w_mid, w_out, b_hid, b_out):
    first_pre = jnp.dot(w_in.T, block, preferred_element_type=jnp.float32) + b_hid[0][:, None]
    first = jax.nn.silu(first_pre).astype(jnp.bfloat16)
    second_pre = jnp.dot(w_mid.T, first, preferred_element_type=jnp.float32) + b_hid[1][:, None]
    second = jax.nn.silu(second_pre).astype(jnp.bfloat16)
    logits = jnp.dot(w_out, second, preferred_element_type=jnp.float32) + b_out[:, None]
    return (first_pre, first, second_pre, second, logits)

def push_solve(rhs, pointer, mult, rounds):
    value = rhs
    for level in range(rounds):
        value = value + jax.ops.segment_sum(mult * value, pointer, num_segments=value.shape[0])
        mult = mult * mult[pointer]
        pointer = pointer[pointer]
    return value

def pull_solve(rhs, pointer, mult, rounds):
    value = rhs
    for level in range(rounds):
        value = value + mult * value[pointer]
        mult = mult * mult[pointer]
        pointer = pointer[pointer]
    return value

def reference(attributes, w_in, w_mid, w_out, b_hid, b_out, downstream, lateral, flow_start, cotangent):
    blocks = REACHES // R_DEV
    stacked = jnp.transpose(attributes.reshape(ATTR, blocks, R_DEV), (1, 0, 2))

    def block_logits(block):
        return layer_forward(block, w_in, w_mid, w_out, b_hid, b_out)[4]
    logits = jnp.transpose(lax.map(block_logits, stacked), (1, 0, 2)).reshape(2, REACHES)
    coeffs, coeff_vjp = jax.vjp(coefficients, logits)
    c_new, c_old, c_self, c_lat = coeffs
    index = jnp.arange(REACHES, dtype=jnp.int32)
    outlet = downstream < 0
    pointer = jnp.where(outlet, index, downstream).astype(jnp.int32)
    live = jnp.where(outlet, 0.0, 1.0)
    mult = jnp.where(outlet, 0.0, c_new[pointer])
    rounds = REACHES.bit_length()

    def inflow_of(values):
        return jax.ops.segment_sum(values * live, pointer, num_segments=REACHES)
    states = [flow_start]
    inflows = [inflow_of(flow_start)]
    for step in range(STEPS):
        rhs = c_old * inflows[-1] + c_self * states[-1] + c_lat * lateral[step]
        flow = push_solve(rhs, pointer, mult, rounds)
        states.append(flow)
        inflows.append(inflow_of(flow))
    grad_new = jnp.zeros((REACHES,), jnp.float32)
    grad_old = jnp.zeros((REACHES,), jnp.float32)
    grad_self = jnp.zeros((REACHES,), jnp.float32)
    grad_lat = jnp.zeros((REACHES,), jnp.float32)
    carry = jnp.zeros((REACHES,), jnp.float32)
    for step in range(STEPS - 1, -1, -1):
        adjoint = pull_solve(cotangent[step] + carry, pointer, mult, rounds)
        grad_new = grad_new + adjoint * inflows[step + 1]
        grad_old = grad_old + adjoint * inflows[step]
        grad_self = grad_self + adjoint * states[step]
        grad_lat = grad_lat + adjoint * lateral[step]
        carry = c_self * adjoint + (c_old * adjoint)[pointer] * live
    grad_logits, = coeff_vjp((grad_new, grad_old, grad_self, grad_lat))
    grad_stacked = jnp.transpose(grad_logits.reshape(2, blocks, R_DEV), (1, 0, 2))

    def accumulate(totals, pieces):
        block, grad_block = pieces
        first_pre, first, second_pre, second, unused = layer_forward(block, w_in, w_mid, w_out, b_hid, b_out)
        logit_bf = grad_block.astype(jnp.bfloat16)
        part_out = contract_last(logit_bf, second)
        pre_two = jnp.dot(w_out.T, logit_bf, preferred_element_type=jnp.float32) * silu_slope(second_pre)
        pre_two_bf = pre_two.astype(jnp.bfloat16)
        part_mid = contract_last(first, pre_two_bf)
        pre_one = jnp.dot(w_mid, pre_two_bf, preferred_element_type=jnp.float32) * silu_slope(first_pre)
        part_in = contract_last(block, pre_one.astype(jnp.bfloat16))
        part_bias = jnp.stack([lax.optimization_barrier(jnp.sum(pre_one, axis=1)), lax.optimization_barrier(jnp.sum(pre_two, axis=1))])
        return ((totals[0] + part_in, totals[1] + part_mid, totals[2] + part_out, totals[3] + part_bias), None)
    start = (jnp.zeros((ATTR, HID), jnp.float32), jnp.zeros((HID, HID), jnp.float32), jnp.zeros((2, HID), jnp.float32), jnp.zeros((2, HID), jnp.float32))
    totals, unused = lax.scan(accumulate, start, (stacked, grad_stacked))
    flows = jnp.stack(states[1:])
    return (flows, totals[0], totals[1], totals[2], totals[3])
```

```python
import functools
import math

import jax
import jax.numpy as jnp
from jax import lax
from jax.experimental import pallas as pl
from jax.experimental.pallas import tpu as pltpu
from jax.sharding import PartitionSpec as P

TIERS = 16
STEPS = 4
RHO_LO = 16.0
RHO_HI = 16000.0
SPAN = math.log(RHO_HI / RHO_LO)
F32 = jnp.float32
BF16 = jnp.bfloat16
CHUNK = 256
MESH = pl.DeviceIdType.MESH


def dot_nn(a, b):
    return lax.dot_general(a, b, (((1,), (0,)), ((), ())), preferred_element_type=F32)


def dot_nt(a, b):
    return lax.dot_general(a, b, (((1,), (1,)), ((), ())), preferred_element_type=F32)


def split(x):
    hi = x.astype(BF16).astype(F32)
    rest = x - hi
    mid = rest.astype(BF16).astype(F32)
    return jnp.concatenate([hi, mid, rest - mid], axis=0).astype(BF16)


def join(y):
    r = y.shape[0] // 3
    return y[:r] + y[r : 2 * r] + y[2 * r : 3 * r]


def onehot(a, b):
    return jnp.where(a == b, 1.0, 0.0).astype(BF16)


def roll_rows(x, by):
    return jnp.concatenate([x[8 - by :], x[: 8 - by]], axis=0)


def poly_tables(coef):
    cols = coef[0].shape[1]
    row = lax.broadcasted_iota(jnp.int32, (8, cols), 0) % 4
    return [jnp.where(row >= k, jnp.broadcast_to(coef[k], (8, cols)), 0.0) for k in range(4)]


def poly_mul(tables, x):
    out = tables[0] * x
    for k in range(1, 4):
        out = out + tables[k] * roll_rows(x, k)
    return out


def sigmoid(v):
    return 1.0 / (1.0 + jnp.exp(-v))


def bit_of(me, b):
    return (me // (1 << b)) % 2


class Stream:
    def __init__(self, me, order, acc, recv, full, ssem, rsem, at):
        self.me, self.order, self.acc, self.recv, self.full = me, order, acc, recv, full
        self.ssem, self.rsem, self.at = ssem, rsem, at
        self.rows = acc.shape[0]
        self.off, self.size, self.slot = 0, self.rows, 0
        self.copy = None

    def partner(self, b):
        return self.me + (1 - 2 * bit_of(self.me, b)) * (1 << b)

    def put(self, src, dst, stage, b):
        self.copy = pltpu.make_async_remote_copy(
            src_ref=src,
            dst_ref=dst,
            send_sem=self.ssem.at[self.at, stage],
            recv_sem=self.rsem.at[self.at, stage],
            device_id={"region": self.partner(b)},
            device_id_type=MESH,
        )
        self.copy.start()

    def scatter_start(self, s):
        b = self.order[s]
        half = self.size // 2
        mine = bit_of(self.me, b)
        give = pl.multiple_of(self.off + (1 - mine) * half, 8)
        self.off = self.off + mine * half
        self.size = half
        self.put(self.acc.at[pl.ds(give, half)], self.recv.at[pl.ds(self.slot, half)], s, b)

    def scatter_end(self, s):
        self.copy.wait()
        own = pl.ds(pl.multiple_of(self.off, 8), self.size)
        total = self.acc[own, :] + self.recv[pl.ds(self.slot, self.size), :]
        self.slot += self.size
        if s == len(self.order) - 1:
            self.full[own, :] = total
        else:
            self.acc[own, :] = total

    def gather_start(self, s):
        b = self.order[len(self.order) - 1 - s]
        own = self.full.at[pl.ds(pl.multiple_of(self.off, 8), self.size)]
        self.put(own, own, len(self.order) + s, b)
        self.off = self.off - bit_of(self.me, b) * self.size
        self.size *= 2

    def gather_end(self, s):
        self.copy.wait()


def kernel(
    n,
    attr_ref, w_in_ref, w_mid_ref, w_out_ref, b_hid_ref, b_out_ref, down_ref, lat_ref, start_ref, cot_ref,
    flows_ref, gin_ref, gmid_ref, gout_ref, gbias_ref,
    pre1, act1, pre2, act2, wmt, grad2, grad1, oh, prior, begun, info, gath, tail_s, tail_r, info_s, info_r,
    acc_a, acc_b, acc_c, rec_a, rec_b, rec_c, full_a, full_b, full_c, red_s, red_r,
):
    rows = down_ref.shape[1]
    hid = w_mid_ref.shape[0]
    exits = rows // TIERS
    tail = rows - exits
    me = lax.axis_index("region")
    base = me * rows

    barrier = pltpu.get_barrier_semaphore()

    def greet(k, c):
        pl.semaphore_signal(barrier, inc=1, device_id={"region": (me + k) % n}, device_id_type=MESH)
        return c

    lax.fori_loop(1, n, greet, 0)
    pl.semaphore_wait(barrier, n - 1)
    onward = (me + 1) % n
    hello = [
        pltpu.make_async_remote_copy(
            src_ref=src, dst_ref=dst, send_sem=tail_s.at[i], recv_sem=tail_r.at[i],
            device_id={"region": onward}, device_id_type=MESH,
        )
        for i, (src, dst) in enumerate(((down_ref, prior), (start_ref, begun)))
    ]
    for copy in hello:
        copy.start()

    columns = jnp.concatenate(
        [b_hid_ref[...], w_out_ref[...].astype(F32), jnp.zeros((4, hid), F32)], axis=0
    ).T
    bias1, bias2 = columns[:, 0:1], columns[:, 1:2]
    w_in_t = w_in_ref[...].T
    wmt[...] = w_mid_ref[...].T

    def forward(c, carry):
        at = pl.ds(pl.multiple_of(c * CHUNK, CHUNK), CHUNK)
        p = dot_nn(w_in_t, attr_ref[:, at]) + bias1
        pre1[:, at] = p
        a = (p * sigmoid(p)).astype(BF16)
        act1[:, at] = a
        q = dot_nn(wmt[...], a) + bias2
        pre2[:, at] = q
        act2[:, at] = (q * sigmoid(q)).astype(BF16)
        return carry

    lax.fori_loop(0, rows // CHUNK, forward, 0)
    logits = dot_nn(w_out_ref[...], act2[...])
    s0 = sigmoid(logits[0:1] + b_out_ref[0])
    s1 = sigmoid(logits[1:2] + b_out_ref[1])
    rho = RHO_LO * jnp.exp(SPAN * s0)
    weight = 0.45 * s1
    denom = rho + 2.0 * (1.0 - weight)
    c_new = (rho - 2.0 * weight) / denom
    c_old = (rho + 2.0 * weight) / denom
    c_self = (2.0 * (1.0 - weight) - rho) / denom
    c_lat = 2.0 * rho / denom

    t1 = c_old + c_self * c_new
    trans = poly_tables([c_new, t1, c_self * t1, c_self * c_self * t1])
    self2 = c_self * c_self
    hold = poly_tables([jnp.ones_like(c_self), c_self, self2, self2 * c_self])

    ptr = down_ref[...] - base
    lane = lax.broadcasted_iota(jnp.int32, (1, rows), 1)
    window = jnp.where(ptr >= tail, ptr - tail + 3 * exits, ptr - exits * (lane // exits + 1))
    slots = lax.broadcasted_iota(jnp.int32, (4 * exits, exits), 0)
    for k in range(TIERS - 1):
        oh[k] = onehot(slots, window[:, k * exits : (k + 1) * exits])

    def tier(x, k):
        return x[:, k * exits : (k + 1) * exits]

    def targets(k):
        return [j if j < TIERS - 1 else None for j in (k + 1, k + 2, k + 3)] + [TIERS - 1]

    cot = cot_ref[...]
    seed = jnp.concatenate([cot[3:4], cot[2:3], cot[1:2], cot[0:1], jnp.zeros((4, rows), F32)], axis=0)
    row8 = lax.broadcasted_iota(jnp.int32, (8, exits), 0)
    pulled = [None] * TIERS
    passed = [None] * TIERS
    exit_of = [None] * TIERS
    stacks = [None] * TIERS
    blank = jnp.zeros((32, exits), BF16)
    for k in range(TIERS - 1, -1, -1):
        if k == TIERS - 1:
            got = jnp.where(row8 == 4, 1.0, 0.0).astype(F32)
            slot = lax.broadcasted_iota(jnp.int32, (8, exits), 1).astype(F32)
        else:
            parts = [blank if j is None else stacks[j] for j in targets(k)]
            res = dot_nn(jnp.concatenate(parts, axis=1), oh[k])
            got = join(res[:24])
            slot = res[24:32]
        pulled[k] = got
        exit_of[k] = slot
        out = poly_mul([tier(x, k) for x in trans], tier(seed, k) + got)
        passed[k] = out
        stacks[k] = jnp.concatenate([split(out), slot.astype(BF16)], axis=0)
    pulled = jnp.concatenate(pulled, axis=1)
    passed = jnp.concatenate(passed, axis=1)
    exit_row = jnp.concatenate(exit_of, axis=1)

    flow0 = start_ref[...]
    wide0 = jnp.broadcast_to(flow0, (8, rows))
    inflow0 = [jnp.zeros((8, exits), F32)] * TIERS
    for k in range(TIERS - 1):
        res = join(dot_nt(split(tier(wide0, k)), oh[k]))
        for p, j in enumerate(targets(k)):
            if j is not None:
                inflow0[j] = inflow0[j] + res[:, p * exits : (p + 1) * exits]
    inflow0 = jnp.concatenate(inflow0, axis=1)

    for copy in hello:
        copy.wait()
    entry = prior[:, tail:] - base
    entry = jnp.where(me > 0, entry, -1)
    enter = onehot(lax.broadcasted_iota(jnp.int32, (rows, exits), 0), entry)
    begun8 = jnp.broadcast_to(begun[:, tail:], (8, exits))
    inflow0 = (inflow0 + join(dot_nt(split(begun8), enter)))[0:1]
    lat = lat_ref[...]
    source = c_lat * lat
    first_source = source[0:1] + c_old * inflow0 + c_self * flow0
    source8 = jnp.concatenate([first_source, source[1:4], jnp.zeros((4, rows), F32)], axis=0)
    local = poly_mul(hold, source8)

    factor = jnp.concatenate([pulled[4:8], jnp.zeros((4, rows), F32)], axis=0)
    factor = poly_tables([factor[k : k + 1] for k in range(4)])
    exit_i = exit_row[0:1].astype(jnp.int32)
    to_exit = onehot(lax.broadcasted_iota(jnp.int32, (exits, rows), 0), exit_i)
    head = join(dot_nt(split(poly_mul(factor, local)), to_exit))
    lead = dot_nn(jnp.concatenate([split(passed), exit_row.astype(BF16)], axis=0), enter)
    packed = jnp.concatenate([join(lead[:24]), head[0:4], lead[24:28]], axis=0)
    packed = jnp.concatenate([packed, jnp.zeros((16, 128 - exits), F32)], axis=1)
    info[...] = packed
    gath[me] = packed

    def tell(k):
        peer = (me + k) % n
        return pltpu.make_async_remote_copy(
            src_ref=info, dst_ref=gath.at[me], send_sem=info_s.at[peer], recv_sem=info_r.at[me],
            device_id={"region": peer}, device_id_type=MESH,
        )

    def tell_start(k, c):
        tell(k).start()
        return c

    def tell_wait(k, c):
        peer = (me + k) % n
        copy = pltpu.make_async_remote_copy(
            src_ref=info, dst_ref=gath.at[peer], send_sem=info_s.at[peer], recv_sem=info_r.at[peer],
            device_id={"region": peer}, device_id_type=MESH,
        )
        copy.wait_send()
        copy.wait_recv()
        return c

    lax.fori_loop(1, n, tell_start, 0)
    lax.fori_loop(1, n, tell_wait, 0)

    side = lax.broadcasted_iota(jnp.int32, (exits, exits), 0)
    zeros4 = jnp.zeros((4, exits), F32)
    zeros8 = jnp.zeros((8, exits), F32)

    def block(i):
        whole = gath[i][:, :exits]
        gain = poly_tables([whole[4 + k : 5 + k] for k in range(4)])
        return whole, gain, onehot(side, whole[12:13].astype(jnp.int32))

    def walk(k, carry):
        arrive, leave, own_arrive, own_leave = carry
        whole, gain, hot = block(k)
        moved = join(dot_nt(split(poly_mul(gain, arrive)), hot))
        arrive = jnp.concatenate([whole[8:12], zeros4], axis=0) + moved
        own_arrive = jnp.where(k + 1 == me, arrive, own_arrive)
        i = n - 1 - k
        whole, gain, hot = block(i)
        fetched = join(dot_nn(split(leave), hot))
        leave = jnp.concatenate([whole[0:4], zeros4], axis=0) + poly_mul(gain, fetched)
        own_leave = jnp.where(i - 1 == me, leave, own_leave)
        return arrive, leave, own_arrive, own_leave

    unused, unused, arrive, leave = lax.fori_loop(0, n - 1, walk, (zeros8, zeros8, zeros8, zeros8))

    remote = join(dot_nn(split(leave), to_exit))
    below = seed + jnp.concatenate([pulled[0:4], jnp.zeros((4, rows), F32)], axis=0) + poly_mul(factor, remote)
    lam = poly_mul(hold, below)

    inside = join(dot_nt(split(arrive), enter))
    inflow = [tier(inside, k) for k in range(TIERS)]
    flow = [None] * TIERS
    for k in range(TIERS):
        out = tier(local, k) + poly_mul([tier(x, k) for x in trans], inflow[k])
        flow[k] = out
        if k < TIERS - 1:
            res = join(dot_nt(split(out), oh[k]))
            for p, j in enumerate(targets(k)):
                if j is not None:
                    inflow[j] = inflow[j] + res[:, p * exits : (p + 1) * exits]
    inflow = jnp.concatenate(inflow, axis=1)
    flow = jnp.concatenate(flow, axis=1)
    flows_ref[...] = flow[0:4]

    dif_new = jnp.zeros((1, rows), F32)
    dif_old = jnp.zeros((1, rows), F32)
    g_lat = jnp.zeros((1, rows), F32)
    for t in range(STEPS):
        adj = lam[3 - t : 4 - t]
        q = flow0 if t == 0 else flow[t - 1 : t]
        i_now = inflow0 if t == 0 else inflow[t - 1 : t]
        dif_new = dif_new + adj * (inflow[t : t + 1] - q)
        dif_old = dif_old + adj * (i_now - q)
        g_lat = g_lat + adj * lat[t : t + 1]
    inv2 = 1.0 / (denom * denom)
    d_rho = (2.0 * dif_new + (2.0 - 4.0 * weight) * dif_old + 4.0 * (1.0 - weight) * g_lat) * inv2
    d_weight = (4.0 * (dif_old - dif_new) + 4.0 * rho * (dif_old + g_lat)) * inv2
    d0 = d_rho * rho * SPAN * s0 * (1.0 - s0)
    d1 = d_weight * 0.45 * s1 * (1.0 - s1)
    logit_bf = jnp.concatenate([d0, d1, jnp.zeros((14, rows), F32)], axis=0).astype(BF16)
    lf = logit_bf.astype(F32)
    info_rows = lf[0:2]
    begun_w = columns
    w0, w1 = begun_w[:, 2:3], begun_w[:, 3:4]

    sum1 = jnp.zeros((hid, 128), F32)
    sum2 = jnp.zeros((hid, 128), F32)
    for c in range(rows // CHUNK):
        at = slice(c * CHUNK, (c + 1) * CHUNK)
        q = pre2[:, at]
        sig = sigmoid(q)
        two = (w0 * info_rows[0:1, at] + w1 * info_rows[1:2, at]) * (sig * (1.0 + q * (1.0 - sig)))
        grad2[:, at] = two.astype(BF16)
        for j in range(0, CHUNK, 128):
            sum2 = sum2 + two[:, j : j + 128]
        p = pre1[:, at]
        sig = sigmoid(p)
        one = dot_nn(w_mid_ref[...], grad2[:, at]) * (sig * (1.0 + p * (1.0 - sig)))
        grad1[:, at] = one.astype(BF16)
        for j in range(0, CHUNK, 128):
            sum1 = sum1 + one[:, j : j + 128]
    half = hid // 2

    def product(c, carry):
        at = pl.ds(pl.multiple_of(c * 128, 128), 128)
        acc_a[at, :] = dot_nt(act1[at, :], grad2[0:half, :])
        acc_b[at, :] = dot_nt(act1[at, :], grad2[half:hid, :])
        return carry

    lax.fori_loop(0, hid // 128, product, 0)
    part_in = dot_nt(attr_ref[...], grad1[...])
    part_out = dot_nt(logit_bf, act2[...])
    bias_rows = [jnp.sum(s.T, axis=0, keepdims=True) for s in (sum1, sum2)]
    last = jnp.concatenate([part_out[0:2]] + bias_rows + [jnp.zeros((4, hid), F32)], axis=0)
    small = [part_in[0:8], part_in[8:16], last]
    tiles = hid // 128
    acc_c[...] = jnp.zeros_like(acc_c)
    for r in range(3):
        for c in range(tiles):
            i = r * tiles + c
            acc_c[8 * i : 8 * i + 8, :] = small[r][:, c * 128 : (c + 1) * 128]

    bits = n.bit_length() - 1
    order = list(range(bits))
    turned = [0] + list(range(2, bits)) + [1]
    streams = [
        Stream(me, order, acc_a, rec_a, full_a, red_s, red_r, 0),
        Stream(me, turned, acc_b, rec_b, full_b, red_s, red_r, 1),
        Stream(me, order, acc_c, rec_c, full_c, red_s, red_r, 2),
    ]
    for s in range(bits):
        for one in streams:
            if s > 0:
                one.scatter_end(s - 1)
            one.scatter_start(s)
    for s in range(bits):
        for one in streams:
            if s > 0:
                one.gather_end(s - 1)
            else:
                one.scatter_end(bits - 1)
            one.gather_start(s)
    for one in streams:
        one.gather_end(bits - 1)
    gmid_ref[:, 0:half] = full_a[...]
    gmid_ref[:, half:hid] = full_b[...]
    for c in range(tiles):
        at = slice(c * 128, (c + 1) * 128)
        gin_ref[0:8, at] = full_c[8 * c : 8 * c + 8, :]
        gin_ref[8:16, at] = full_c[8 * (tiles + c) : 8 * (tiles + c) + 8, :]
        final = full_c[8 * (2 * tiles + c) : 8 * (2 * tiles + c) + 8, :]
        gout_ref[:, at] = final[0:2]
        gbias_ref[:, at] = final[2:4]


def body(n, attributes, w_in, w_mid, w_out, b_hid, b_out, downstream, lateral, flow_start, cotangent):
    rows = downstream.shape[0]
    hid = w_mid.shape[0]
    attrs = w_in.shape[0]
    exits = rows // TIERS
    half = hid // 2
    bits = n.bit_length() - 1
    vmem = pl.BlockSpec(memory_space=pltpu.VMEM)
    smem = pl.BlockSpec(memory_space=pltpu.SMEM)
    wide = [pltpu.VMEM((hid, half), F32)] * 2 + [pltpu.VMEM((8 * n, 128), F32)]
    flops = 2 * rows * hid * (3 * hid + 4 * attrs)
    return pl.pallas_call(
        functools.partial(kernel, n),
        out_shape=(
            jax.ShapeDtypeStruct((STEPS, rows), F32),
            jax.ShapeDtypeStruct((attrs, hid), F32),
            jax.ShapeDtypeStruct((hid, hid), F32),
            jax.ShapeDtypeStruct((2, hid), F32),
            jax.ShapeDtypeStruct((2, hid), F32),
        ),
        in_specs=[vmem] * 5 + [smem] + [vmem] * 4,
        out_specs=(vmem,) * 5,
        scratch_shapes=[
            pltpu.VMEM((hid, rows), F32),
            pltpu.VMEM((hid, rows), BF16),
            pltpu.VMEM((hid, rows), F32),
            pltpu.VMEM((hid, rows), BF16),
            pltpu.VMEM((hid, hid), BF16),
            pltpu.VMEM((hid, rows), BF16),
            pltpu.VMEM((hid, rows), BF16),
            pltpu.VMEM((TIERS - 1, 4 * exits, exits), BF16),
            pltpu.VMEM((1, rows), jnp.int32),
            pltpu.VMEM((1, rows), F32),
            pltpu.VMEM((16, 128), F32),
            pltpu.VMEM((n, 16, 128), F32),
            pltpu.SemaphoreType.DMA((2,)),
            pltpu.SemaphoreType.DMA((2,)),
            pltpu.SemaphoreType.DMA((n,)),
            pltpu.SemaphoreType.DMA((n,)),
        ]
        + wide * 3
        + [pltpu.SemaphoreType.DMA((3, 2 * bits)), pltpu.SemaphoreType.DMA((3, 2 * bits))],
        compiler_params=pltpu.CompilerParams(
            collective_id=0, has_side_effects=True, vmem_limit_bytes=48 * 1024 * 1024
        ),
        cost_estimate=pl.CostEstimate(flops=flops, bytes_accessed=4 << 20, transcendentals=4 * rows * hid),
    )(
        attributes, w_in, w_mid, w_out, b_hid, b_out,
        downstream.reshape(1, rows), lateral, flow_start.reshape(1, rows), cotangent,
    )


def solution(mesh):
    n = mesh.shape["region"]
    in_specs = (
        P(None, "region"),
        P(),
        P(),
        P(),
        P(),
        P(),
        P("region"),
        P(None, ("groups", "region")),
        P(("groups", "region")),
        P(None, ("groups", "region")),
    )
    out_specs = (
        P(None, ("groups", "region")),
        P("groups", None),
        P("groups", None),
        P("groups", None),
        P("groups", None),
    )
    return jax.shard_map(
        functools.partial(body, n), mesh=mesh, in_specs=in_specs, out_specs=out_specs, check_vma=False
    )
```

```python
import functools
import math

import jax
import jax.numpy as jnp
from jax import lax
from jax.experimental import pallas as pl
from jax.experimental.pallas import tpu as pltpu
from jax.sharding import PartitionSpec as P

TIERS = 16
STEPS = 4
RHO_LO = 16.0
RHO_HI = 16000.0
SPAN = math.log(RHO_HI / RHO_LO)
F32 = jnp.float32
BF16 = jnp.bfloat16
CHUNK = 256
CUTS = 4
MESH = pl.DeviceIdType.MESH


def dot_nn(a, b):
    return lax.dot_general(a, b, (((1,), (0,)), ((), ())), preferred_element_type=F32)


def dot_nt(a, b):
    return lax.dot_general(a, b, (((1,), (1,)), ((), ())), preferred_element_type=F32)


def split(x):
    hi = x.astype(BF16).astype(F32)
    rest = x - hi
    mid = rest.astype(BF16).astype(F32)
    return jnp.concatenate([hi, mid, rest - mid], axis=0).astype(BF16)


def join(y):
    r = y.shape[0] // 3
    return y[:r] + y[r : 2 * r] + y[2 * r : 3 * r]


def onehot(a, b):
    return jnp.where(a == b, 1.0, 0.0).astype(BF16)


def roll_rows(x, by):
    return jnp.concatenate([x[8 - by :], x[: 8 - by]], axis=0)


def poly_tables(coef):
    cols = coef[0].shape[1]
    row = lax.broadcasted_iota(jnp.int32, (8, cols), 0) % 4
    return [jnp.where(row >= k, jnp.broadcast_to(coef[k], (8, cols)), 0.0) for k in range(4)]


def poly_mul(tables, x):
    out = tables[0] * x
    for k in range(1, 4):
        out = out + tables[k] * roll_rows(x, k)
    return out


def sigmoid(v):
    return 1.0 / (1.0 + jnp.exp(-v))


class Stream:
    def __init__(self, me, order, acc, recv, full, ssem, rsem, at):
        self.me, self.order, self.acc, self.recv, self.full = me, order, acc, recv, full
        self.ssem, self.rsem, self.at, self.sem = ssem, rsem, at, 0
        self.off, self.size, self.slot = 0, acc.shape[0], 0
        self.copies, self.sent = [], []

    def digit(self, group):
        return (self.me // (1 << group[0])) % (1 << len(group))

    def put(self, src, dst, peer):
        copy = pltpu.make_async_remote_copy(
            src_ref=src,
            dst_ref=dst,
            send_sem=self.ssem.at[self.at, self.sem],
            recv_sem=self.rsem.at[self.at, self.sem],
            device_id={"region": peer},
            device_id_type=MESH,
        )
        copy.start()
        self.sem += 1
        self.copies.append(copy)
        self.sent.append(copy)

    def arrived(self):
        for copy in self.copies:
            copy.wait_recv()
        self.copies = []

    def scatter_start(self, s):
        group = self.order[s]
        ways, mine = 1 << len(group), self.digit(group)
        self.size //= ways
        for k in range(1, ways):
            other = (mine + k) % ways
            give = pl.ds(pl.multiple_of(self.off + other * self.size, 8), self.size)
            slot = pl.ds(self.slot + (k - 1) * self.size, self.size)
            self.put(self.acc.at[give], self.recv.at[slot], self.me + (other - mine) * (1 << group[0]))
        self.off = self.off + mine * self.size

    def scatter_end(self, s):
        self.arrived()
        own = pl.ds(pl.multiple_of(self.off, 8), self.size)
        total = self.acc[own, :]
        for k in range(1, 1 << len(self.order[s])):
            total = total + self.recv[pl.ds(self.slot, self.size), :]
            self.slot += self.size
        if s == len(self.order) - 1:
            self.full[own, :] = total
        else:
            self.acc[own, :] = total

    def gather_start(self, s):
        group = self.order[len(self.order) - 1 - s]
        ways, mine = 1 << len(group), self.digit(group)
        own = self.full.at[pl.ds(pl.multiple_of(self.off, 8), self.size)]
        for k in range(1, ways):
            other = (mine + k) % ways
            self.put(own, own, self.me + (other - mine) * (1 << group[0]))
        self.off = self.off - mine * self.size
        self.size *= ways

    def gather_end(self, s):
        self.arrived()

    def finish(self):
        for copy in self.sent:
            copy.wait_send()


def groups_of(n):
    bits = n.bit_length() - 1
    rest = [tuple(range(b, min(b + 2, bits))) for b in range(2, bits, 2)]
    return [(0,), (1,)] + rest, [(0,)] + rest + [(1,)]


def kernel(
    n,
    attr_hbm, w_in_hbm, w_mid_hbm, w_out_ref, b_hid_hbm, b_out_ref, down_hbm, lat_hbm, start_hbm, cot_hbm,
    flows_ref, gin_ref, gmid_ref, gout_ref, gbias_ref,
    pre1, act1, pre2, act2, wmt, grad2, grad1, oh, prior, begun, info, gath, tail_s, tail_r, info_s, info_r,
    attr_ref, w_in_ref, w_mid_ref, b_hid_ref, down_ref, lat_ref, start_ref, cot_ref, load_s,
    acc, rec, full, acc_c, rec_c, full_c, red_s, red_r,
):
    loads = [
        pltpu.make_async_copy(src, dst, load_s.at[i])
        for i, (src, dst) in enumerate(
            (
                (down_hbm, down_ref),
                (start_hbm, start_ref),
                (w_mid_hbm, w_mid_ref),
                (attr_hbm, attr_ref),
                (w_in_hbm, w_in_ref),
                (b_hid_hbm, b_hid_ref),
                (lat_hbm, lat_ref),
                (cot_hbm, cot_ref),
            )
        )
    ]
    for load in loads:
        load.start()
    rows = down_ref.shape[1]
    hid = w_mid_ref.shape[0]
    exits = rows // TIERS
    tail = rows - exits
    me = lax.axis_index("region")
    base = me * rows

    barrier = pltpu.get_barrier_semaphore()

    def greet(k, c):
        pl.semaphore_signal(barrier, inc=1, device_id={"region": (me + k) % n}, device_id_type=MESH)
        return c

    lax.fori_loop(1, n, greet, 0)
    pl.semaphore_wait(barrier, n - 1)
    onward = (me + 1) % n
    hello = [
        pltpu.make_async_remote_copy(
            src_ref=src, dst_ref=dst, send_sem=tail_s.at[i], recv_sem=tail_r.at[i],
            device_id={"region": onward}, device_id_type=MESH,
        )
        for i, (src, dst) in enumerate(((down_ref, prior), (start_ref, begun)))
    ]
    for load in loads[:2]:
        load.wait()
    for copy in hello:
        copy.start()
    for load in loads[2:]:
        load.wait()

    columns = jnp.concatenate(
        [b_hid_ref[...], w_out_ref[...].astype(F32), jnp.zeros((4, hid), F32)], axis=0
    ).T
    bias1, bias2 = columns[:, 0:1], columns[:, 1:2]
    w_in_t = w_in_ref[...].T
    wmt[...] = w_mid_ref[...].T

    def forward(c, carry):
        at = pl.ds(pl.multiple_of(c * CHUNK, CHUNK), CHUNK)
        p = dot_nn(w_in_t, attr_ref[:, at]) + bias1
        pre1[:, at] = p
        a = (p * sigmoid(p)).astype(BF16)
        act1[:, at] = a
        q = dot_nn(wmt[...], a) + bias2
        pre2[:, at] = q
        act2[:, at] = (q * sigmoid(q)).astype(BF16)
        return carry

    lax.fori_loop(0, rows // CHUNK, forward, 0)
    logits = dot_nn(w_out_ref[...], act2[...])
    s0 = sigmoid(logits[0:1] + b_out_ref[0])
    s1 = sigmoid(logits[1:2] + b_out_ref[1])
    rho = RHO_LO * jnp.exp(SPAN * s0)
    weight = 0.45 * s1
    denom = rho + 2.0 * (1.0 - weight)
    c_new = (rho - 2.0 * weight) / denom
    c_old = (rho + 2.0 * weight) / denom
    c_self = (2.0 * (1.0 - weight) - rho) / denom
    c_lat = 2.0 * rho / denom

    t1 = c_old + c_self * c_new
    trans = poly_tables([c_new, t1, c_self * t1, c_self * c_self * t1])
    self2 = c_self * c_self
    hold = poly_tables([jnp.ones_like(c_self), c_self, self2, self2 * c_self])

    ptr = down_ref[...] - base
    lane = lax.broadcasted_iota(jnp.int32, (1, rows), 1)
    window = jnp.where(ptr >= tail, ptr - tail + 3 * exits, ptr - exits * (lane // exits + 1))
    slots = lax.broadcasted_iota(jnp.int32, (4 * exits, exits), 0)
    for k in range(TIERS - 1):
        oh[k] = onehot(slots, window[:, k * exits : (k + 1) * exits])

    def tier(x, k):
        return x[:, k * exits : (k + 1) * exits]

    def targets(k):
        return [j if j < TIERS - 1 else None for j in (k + 1, k + 2, k + 3)] + [TIERS - 1]

    cot = cot_ref[...]
    seed = jnp.concatenate([cot[3:4], cot[2:3], cot[1:2], cot[0:1], jnp.zeros((4, rows), F32)], axis=0)
    row8 = lax.broadcasted_iota(jnp.int32, (8, exits), 0)
    pulled = [None] * TIERS
    passed = [None] * TIERS
    exit_of = [None] * TIERS
    stacks = [None] * TIERS
    blank = jnp.zeros((32, exits), BF16)
    for k in range(TIERS - 1, -1, -1):
        if k == TIERS - 1:
            got = jnp.where(row8 == 4, 1.0, 0.0).astype(F32)
            slot = lax.broadcasted_iota(jnp.int32, (8, exits), 1).astype(F32)
        else:
            parts = [blank if j is None else stacks[j] for j in targets(k)]
            res = dot_nn(jnp.concatenate(parts, axis=1), oh[k])
            got = join(res[:24])
            slot = res[24:32]
        pulled[k] = got
        exit_of[k] = slot
        out = poly_mul([tier(x, k) for x in trans], tier(seed, k) + got)
        passed[k] = out
        stacks[k] = jnp.concatenate([split(out), slot.astype(BF16)], axis=0)
    pulled = jnp.concatenate(pulled, axis=1)
    passed = jnp.concatenate(passed, axis=1)
    exit_row = jnp.concatenate(exit_of, axis=1)

    flow0 = start_ref[...]
    wide0 = jnp.broadcast_to(flow0, (8, rows))
    inflow0 = [jnp.zeros((8, exits), F32)] * TIERS
    for k in range(TIERS - 1):
        res = join(dot_nt(split(tier(wide0, k)), oh[k]))
        for p, j in enumerate(targets(k)):
            if j is not None:
                inflow0[j] = inflow0[j] + res[:, p * exits : (p + 1) * exits]
    inflow0 = jnp.concatenate(inflow0, axis=1)

    for copy in hello:
        copy.wait()
    entry = prior[:, tail:] - base
    entry = jnp.where(me > 0, entry, -1)
    enter = onehot(lax.broadcasted_iota(jnp.int32, (rows, exits), 0), entry)
    begun8 = jnp.broadcast_to(begun[:, tail:], (8, exits))
    inflow0 = (inflow0 + join(dot_nt(split(begun8), enter)))[0:1]
    lat = lat_ref[...]
    source = c_lat * lat
    first_source = source[0:1] + c_old * inflow0 + c_self * flow0
    source8 = jnp.concatenate([first_source, source[1:4], jnp.zeros((4, rows), F32)], axis=0)
    local = poly_mul(hold, source8)

    factor = jnp.concatenate([pulled[4:8], jnp.zeros((4, rows), F32)], axis=0)
    factor = poly_tables([factor[k : k + 1] for k in range(4)])
    exit_i = exit_row[0:1].astype(jnp.int32)
    to_exit = onehot(lax.broadcasted_iota(jnp.int32, (exits, rows), 0), exit_i)
    head = join(dot_nt(split(poly_mul(factor, local)), to_exit))
    lead = dot_nn(jnp.concatenate([split(passed), exit_row.astype(BF16)], axis=0), enter)
    packed = jnp.concatenate([join(lead[:24]), head[0:4], lead[24:28]], axis=0)
    packed = jnp.concatenate([packed, jnp.zeros((16, 128 - exits), F32)], axis=1)
    info[...] = packed
    gath[me] = packed

    def tell(k):
        peer = (me + k) % n
        return pltpu.make_async_remote_copy(
            src_ref=info, dst_ref=gath.at[me], send_sem=info_s.at[peer], recv_sem=info_r.at[me],
            device_id={"region": peer}, device_id_type=MESH,
        )

    def tell_start(k, c):
        tell(k).start()
        return c

    def tell_wait(k, c):
        peer = (me + k) % n
        copy = pltpu.make_async_remote_copy(
            src_ref=info, dst_ref=gath.at[peer], send_sem=info_s.at[peer], recv_sem=info_r.at[peer],
            device_id={"region": peer}, device_id_type=MESH,
        )
        copy.wait_send()
        copy.wait_recv()
        return c

    lax.fori_loop(1, n, tell_start, 0)
    lax.fori_loop(1, n, tell_wait, 0)

    side = lax.broadcasted_iota(jnp.int32, (exits, exits), 0)
    zeros4 = jnp.zeros((4, exits), F32)
    zeros8 = jnp.zeros((8, exits), F32)

    def block(i):
        whole = gath[i][:, :exits]
        gain = poly_tables([whole[4 + k : 5 + k] for k in range(4)])
        return whole, gain, onehot(side, whole[12:13].astype(jnp.int32))

    def walk(k, carry):
        arrive, leave, own_arrive, own_leave = carry
        whole, gain, hot = block(k)
        moved = join(dot_nt(split(poly_mul(gain, arrive)), hot))
        arrive = jnp.concatenate([whole[8:12], zeros4], axis=0) + moved
        own_arrive = jnp.where(k + 1 == me, arrive, own_arrive)
        i = n - 1 - k
        whole, gain, hot = block(i)
        fetched = join(dot_nn(split(leave), hot))
        leave = jnp.concatenate([whole[0:4], zeros4], axis=0) + poly_mul(gain, fetched)
        own_leave = jnp.where(i - 1 == me, leave, own_leave)
        return arrive, leave, own_arrive, own_leave

    unused, unused, arrive, leave = lax.fori_loop(0, n - 1, walk, (zeros8, zeros8, zeros8, zeros8))

    remote = join(dot_nn(split(leave), to_exit))
    below = seed + jnp.concatenate([pulled[0:4], jnp.zeros((4, rows), F32)], axis=0) + poly_mul(factor, remote)
    lam = poly_mul(hold, below)

    inside = join(dot_nt(split(arrive), enter))
    inflow = [tier(inside, k) for k in range(TIERS)]
    flow = [None] * TIERS
    for k in range(TIERS):
        out = tier(local, k) + poly_mul([tier(x, k) for x in trans], inflow[k])
        flow[k] = out
        if k < TIERS - 1:
            res = join(dot_nt(split(out), oh[k]))
            for p, j in enumerate(targets(k)):
                if j is not None:
                    inflow[j] = inflow[j] + res[:, p * exits : (p + 1) * exits]
    inflow = jnp.concatenate(inflow, axis=1)
    flow = jnp.concatenate(flow, axis=1)
    flows_ref[...] = flow[0:4]

    dif_new = jnp.zeros((1, rows), F32)
    dif_old = jnp.zeros((1, rows), F32)
    g_lat = jnp.zeros((1, rows), F32)
    for t in range(STEPS):
        adj = lam[3 - t : 4 - t]
        q = flow0 if t == 0 else flow[t - 1 : t]
        i_now = inflow0 if t == 0 else inflow[t - 1 : t]
        dif_new = dif_new + adj * (inflow[t : t + 1] - q)
        dif_old = dif_old + adj * (i_now - q)
        g_lat = g_lat + adj * lat[t : t + 1]
    inv2 = 1.0 / (denom * denom)
    d_rho = (2.0 * dif_new + (2.0 - 4.0 * weight) * dif_old + 4.0 * (1.0 - weight) * g_lat) * inv2
    d_weight = (4.0 * (dif_old - dif_new) + 4.0 * rho * (dif_old + g_lat)) * inv2
    d0 = d_rho * rho * SPAN * s0 * (1.0 - s0)
    d1 = d_weight * 0.45 * s1 * (1.0 - s1)
    logit_bf = jnp.concatenate([d0, d1, jnp.zeros((14, rows), F32)], axis=0).astype(BF16)
    lf = logit_bf.astype(F32)
    info_rows = lf[0:2]
    begun_w = columns
    w0, w1 = begun_w[:, 2:3], begun_w[:, 3:4]

    sum1 = jnp.zeros((hid, 128), F32)
    sum2 = jnp.zeros((hid, 128), F32)
    for c in range(rows // CHUNK):
        at = slice(c * CHUNK, (c + 1) * CHUNK)
        q = pre2[:, at]
        sig = sigmoid(q)
        two = (w0 * info_rows[0:1, at] + w1 * info_rows[1:2, at]) * (sig * (1.0 + q * (1.0 - sig)))
        grad2[:, at] = two.astype(BF16)
        for j in range(0, CHUNK, 128):
            sum2 = sum2 + two[:, j : j + 128]
        p = pre1[:, at]
        sig = sigmoid(p)
        one = dot_nn(w_mid_ref[...], grad2[:, at]) * (sig * (1.0 + p * (1.0 - sig)))
        grad1[:, at] = one.astype(BF16)
        for j in range(0, CHUNK, 128):
            sum1 = sum1 + one[:, j : j + 128]
    wide = hid // CUTS

    def product(c, carry):
        at = pl.ds(pl.multiple_of(c * 128, 128), 128)
        both = dot_nt(act1[at, :], grad2[...])
        for i in range(CUTS):
            acc[i, at, :] = both[:, i * wide : (i + 1) * wide]
        return carry

    lax.fori_loop(0, hid // 128, product, 0)
    part_in = dot_nt(attr_ref[...], grad1[...])
    part_out = dot_nt(logit_bf, act2[...])
    bias_rows = [jnp.sum(s.T, axis=0, keepdims=True) for s in (sum1, sum2)]
    last = jnp.concatenate([part_out[0:2]] + bias_rows + [jnp.zeros((4, hid), F32)], axis=0)
    small = [part_in[0:8], part_in[8:16], last]
    tiles = hid // 128
    acc_c[...] = jnp.zeros_like(acc_c)
    for r in range(3):
        for c in range(tiles):
            i = r * tiles + c
            acc_c[8 * i : 8 * i + 8, :] = small[r][:, c * 128 : (c + 1) * 128]

    order, turned = groups_of(n)
    stages = len(order)
    streams = [
        Stream(me, turned if i % 4 == 1 else order, acc.at[i], rec.at[i], full.at[i], red_s, red_r, i)
        for i in range(CUTS)
    ] + [Stream(me, order, acc_c, rec_c, full_c, red_s, red_r, CUTS)]
    for s in range(stages):
        for one in streams:
            if s > 0:
                one.scatter_end(s - 1)
            one.scatter_start(s)
    for s in range(stages):
        for one in streams:
            if s > 0:
                one.gather_end(s - 1)
            else:
                one.scatter_end(stages - 1)
            one.gather_start(s)
    for one in streams:
        one.gather_end(stages - 1)
    for one in streams:
        one.finish()
    for i in range(CUTS):
        gmid_ref[:, i * wide : (i + 1) * wide] = full[i]
    for c in range(tiles):
        at = slice(c * 128, (c + 1) * 128)
        gin_ref[0:8, at] = full_c[8 * c : 8 * c + 8, :]
        gin_ref[8:16, at] = full_c[8 * (tiles + c) : 8 * (tiles + c) + 8, :]
        final = full_c[8 * (2 * tiles + c) : 8 * (2 * tiles + c) + 8, :]
        gout_ref[:, at] = final[0:2]
        gbias_ref[:, at] = final[2:4]


def body(n, attributes, w_in, w_mid, w_out, b_hid, b_out, downstream, lateral, flow_start, cotangent):
    rows = downstream.shape[0]
    hid = w_mid.shape[0]
    attrs = w_in.shape[0]
    exits = rows // TIERS
    sends = 2 * sum((1 << len(group)) - 1 for group in groups_of(n)[0])
    vmem = pl.BlockSpec(memory_space=pltpu.VMEM)
    hbm = pl.BlockSpec(memory_space=pltpu.HBM)
    smem = pl.BlockSpec(memory_space=pltpu.SMEM)
    wide = [pltpu.VMEM((CUTS, hid, hid // CUTS), F32)] * 3 + [pltpu.VMEM((8 * n, 128), F32)] * 3
    flops = 2 * rows * hid * (3 * hid + 4 * attrs)
    return pl.pallas_call(
        functools.partial(kernel, n),
        out_shape=(
            jax.ShapeDtypeStruct((STEPS, rows), F32),
            jax.ShapeDtypeStruct((attrs, hid), F32),
            jax.ShapeDtypeStruct((hid, hid), F32),
            jax.ShapeDtypeStruct((2, hid), F32),
            jax.ShapeDtypeStruct((2, hid), F32),
        ),
        in_specs=[hbm] * 3 + [vmem, hbm, smem] + [hbm] * 4,
        out_specs=(vmem,) * 5,
        scratch_shapes=[
            pltpu.VMEM((hid, rows), F32),
            pltpu.VMEM((hid, rows), BF16),
            pltpu.VMEM((hid, rows), F32),
            pltpu.VMEM((hid, rows), BF16),
            pltpu.VMEM((hid, hid), BF16),
            pltpu.VMEM((hid, rows), BF16),
            pltpu.VMEM((hid, rows), BF16),
            pltpu.VMEM((TIERS - 1, 4 * exits, exits), BF16),
            pltpu.VMEM((1, rows), jnp.int32),
            pltpu.VMEM((1, rows), F32),
            pltpu.VMEM((16, 128), F32),
            pltpu.VMEM((n, 16, 128), F32),
            pltpu.SemaphoreType.DMA((2,)),
            pltpu.SemaphoreType.DMA((2,)),
            pltpu.SemaphoreType.DMA((n,)),
            pltpu.SemaphoreType.DMA((n,)),
            pltpu.VMEM((attrs, rows), BF16),
            pltpu.VMEM((attrs, hid), BF16),
            pltpu.VMEM((hid, hid), BF16),
            pltpu.VMEM((2, hid), F32),
            pltpu.VMEM((1, rows), jnp.int32),
            pltpu.VMEM((STEPS, rows), F32),
            pltpu.VMEM((1, rows), F32),
            pltpu.VMEM((STEPS, rows), F32),
            pltpu.SemaphoreType.DMA((8,)),
        ]
        + wide
        + [pltpu.SemaphoreType.DMA((CUTS + 1, sends)), pltpu.SemaphoreType.DMA((CUTS + 1, sends))],
        compiler_params=pltpu.CompilerParams(
            collective_id=0, has_side_effects=True, vmem_limit_bytes=60 * 1024 * 1024
        ),
        cost_estimate=pl.CostEstimate(flops=flops, bytes_accessed=4 << 20, transcendentals=4 * rows * hid),
    )(
        attributes, w_in, w_mid, w_out, b_hid, b_out,
        downstream.reshape(1, rows), lateral, flow_start.reshape(1, rows), cotangent,
    )


def solution(mesh):
    n = mesh.shape["region"]
    in_specs = (
        P(None, "region"),
        P(),
        P(),
        P(),
        P(),
        P(),
        P("region"),
        P(None, ("groups", "region")),
        P(("groups", "region")),
        P(None, ("groups", "region")),
    )
    out_specs = (
        P(None, ("groups", "region")),
        P("groups", None),
        P("groups", None),
        P("groups", None),
        P("groups", None),
    )
    return jax.shard_map(
        functools.partial(body, n), mesh=mesh, in_specs=in_specs, out_specs=out_specs, check_vma=False
    )
```
